32 devices in a mesh: obs: 4 (over y, x), space: 8 (over z, core).
Axes of the slice: x: 2, y: 2, z: 4, core: 2. Of those that a mesh axis runs over, the one named last changes fastest.
Arguments:
- probes: float32 [32, 4, 128, 256], P(None, None, 'space'), may hold values from -6 to 6
- wind: float32 [4, 2, 2, 4, 128, 256], P('obs', None, None, None, 'space'), may hold values from -0.6 to 0.6
- station_cell: int32 [4, 2048], P('obs', 'space'), may hold values from 0 to 16383
- obs_count: int32 [4, 8], P('obs', 'space'), may hold values from 1 to 256, as said below
- obs_weight: float32 [4, 2048], P('obs', 'space'), may hold values from 0.5 to 4
Outputs:
- basis: float32 [32, 4, 128, 256], P('obs', None, 'space')
- core: float32 [32, 32], replicated
The draws below stay inside these ranges and needn't reach their ends.
Inputs may be any that keep to these rules, and one draw needn't show every extreme that they name: `obs_count`: the live slots of a tile in a window are its first ones; some tile of some window has all 256 live.
All inputs are finite; a program needn't handle non-finite values.
Results may differ from the reference program's by a relative error of at most 0.0003.
Values sent between devices are 32-bit elements; how exact they have to be, the bound alone decides.
A program may use at most 64 MiB of HBM per device.

```python
import math
import jax
import jax.numpy as jnp
from jax import lax

RX = 16
NY = 256
LEV = 4
PROBES = 32
STEPS = 2
SLOTS = 256
NX = 128
GROUPS = 4
TILES = 8
N_SPACE = 8


def draw_obs_count(key, part):
    first_key = jax.random.fold_in(key, 11)
    second_key = jax.random.fold_in(key, 23)
    raw = jax.random.randint(first_key, (GROUPS, TILES), 1, SLOTS + 1)
    counts = jnp.maximum(1, raw * raw // SLOTS).reshape(-1)
    spot = jax.random.randint(second_key, (), 0, GROUPS * TILES)
    counts = counts.at[spot].set(SLOTS)
    return counts.reshape(GROUPS, TILES).astype(jnp.int32)


def plant(values, key, smallest, top_value):
    dims = values.shape
    spot = [jax.random.randint(jax.random.fold_in(key, axis), (), 0, dims[axis]) for axis in range(len(dims))]
    values = values.at[tuple(spot)].set(smallest)
    longest = dims.index(max(dims))
    spot[longest] = (spot[longest] + 1) % dims[longest]
    return values.at[tuple(spot)].set(top_value)


def block_scale(own_key, dims, shards, least, top_value):
    factor_of = 1.0
    for position, blocks in shards:
        draws = jax.random.uniform(jax.random.fold_in(jax.random.fold_in(own_key, 6), position), (blocks,), jnp.float32, least / len(shards), top_value / len(shards))
        factor_of = factor_of * jnp.repeat(jnp.exp(draws), dims[position] // blocks).reshape((-1,) + (1,) * (len(dims) - 1 - position))
    return factor_of


def centred(key, dims, deviation, reach, cuts=(), held_as=jnp.bfloat16):
    values = jax.random.normal(key, dims, jnp.float32) * deviation
    if len(cuts) > 0:
        values = block_scale(key, dims, cuts, -0.22, 0.18) * values
    return jnp.clip(values, min=-reach, max=reach).astype(held_as)


def setup_inputs(seed: int = 0) -> dict:
    streams_of = jax.random.split(jax.random.key(seed), 6)
    probes = centred(streams_of[0], (PROBES, LEV, NX, NY), 1.0, 6.0, ((2, 8),), jnp.float32)
    wind = jnp.clip(jax.random.uniform(streams_of[1], (GROUPS, STEPS, 2, LEV, NX, NY), jnp.float32, -0.6, 0.6) * block_scale(streams_of[1], (GROUPS, STEPS, 2, LEV, NX, NY), ((0, 4), (4, 8)), -0.4, 0.0), -0.6, 0.6)
    station_cell = plant(jax.random.randint(streams_of[2], (GROUPS, TILES * SLOTS), 0, LEV * RX * NY), jax.random.fold_in(streams_of[2], 1), 0, (LEV * RX * NY) - 1).astype(jnp.int32)
    obs_count = draw_obs_count(jax.random.fold_in(streams_of[5], 71), 0)
    obs_weight = jnp.clip(jnp.exp(math.log(4.0) - 2.0794415 * jax.random.uniform(streams_of[4], (GROUPS, TILES * SLOTS), jnp.float32) ** block_scale(streams_of[4], (GROUPS, TILES * SLOTS), ((0, 4), (1, 8)), -0.2, 0.2)), 0.5, 4.0)
    return {"probes": probes, "wind": wind, "station_cell": station_cell, "obs_count": obs_count, "obs_weight": obs_weight}


def pad_rows(field):
    return jnp.pad(field, [(0, 0)] * (field.ndim - 2) + [(1, 1), (0, 0)])

def smooth_terms(centre, upper, lower):
    yplus = jnp.pad(centre, [(0, 0), (0, 0), (0, 0), (0, 1)])[:, :, :, 1:]
    yminus = jnp.pad(centre, [(0, 0), (0, 0), (0, 0), (1, 0)])[:, :, :, :-1]
    zplus = jnp.pad(centre, [(0, 0), (0, 1), (0, 0), (0, 0)])[:, 1:]
    zminus = jnp.pad(centre, [(0, 0), (1, 0), (0, 0), (0, 0)])[:, :-1]
    return (centre + 0.15 * (upper + lower + yplus + yminus - 4.0 * centre) + 0.1 * (zplus + zminus - 2.0 * centre), yplus, yminus)

def forward_advance(extended, wind_x, wind_y):
    centre = extended[:, :, 1:-1]
    upper = extended[:, :, 2:]
    lower = extended[:, :, :-2]
    result, yplus, yminus = smooth_terms(centre, upper, lower)
    return result - 0.5 * (wind_x * (upper - lower) + wind_y * (yplus - yminus))

def adjoint_advance(extended, wind_x_ext, wind_y):
    centre = extended[:, :, 1:-1]
    upper = extended[:, :, 2:]
    lower = extended[:, :, :-2]
    result, yplus, yminus = smooth_terms(centre, upper, lower)
    carried = wind_x_ext * extended
    across = wind_y * centre
    aplus = jnp.pad(across, [(0, 0), (0, 0), (0, 0), (0, 1)])[:, :, :, 1:]
    aminus = jnp.pad(across, [(0, 0), (0, 0), (0, 0), (1, 0)])[:, :, :, :-1]
    return result + 0.5 * (carried[:, :, 2:] - carried[:, :, :-2] + (aplus - aminus))

def reference(probes, wind, station_cell, obs_count, obs_weight):
    slot_ids = jnp.arange(N_SPACE * SLOTS, dtype=jnp.int32)
    tile_ids = (slot_ids // SLOTS).astype(jnp.int32)
    slot_in = (slot_ids % SLOTS).astype(jnp.int32)

    def one_group(total, inputs):
        wind_g, cells_g, count_g, weight_g = inputs
        field = probes
        for step in range(STEPS):
            field = forward_advance(pad_rows(field), wind_g[step, 0], wind_g[step, 1])
        level = cells_g // (RX * NY)
        rest = cells_g % (RX * NY)
        row_glob = tile_ids * RX + rest // NY
        column = rest % NY
        flat_index = ((level * NX + row_glob) * NY + column).astype(jnp.int32)
        live = (slot_in < count_g[tile_ids]).astype(probes.dtype)
        flat = field.reshape(PROBES, -1)
        sampled = flat[:, flat_index]
        weighted = sampled * (weight_g * live)[None, :]
        back = jnp.zeros_like(flat).at[:, flat_index].add(weighted).reshape(probes.shape)
        for step in reversed(range(STEPS)):
            back = adjoint_advance(pad_rows(back), pad_rows(wind_g[step, 0]), wind_g[step, 1])
        return (total + back, None)
    total, _ = lax.scan(one_group, jnp.zeros_like(probes), (wind, station_cell, obs_count, obs_weight))
    sketch = total.reshape(PROBES, -1)
    omega = probes.reshape(PROBES, -1)
    gram = jnp.dot(sketch, sketch.T, precision=lax.Precision.HIGHEST)
    core = jnp.dot(omega, sketch.T, precision=lax.Precision.HIGHEST) / (GROUPS * N_SPACE * SLOTS)
    lower = jnp.linalg.cholesky(gram)
    basis = jax.scipy.linalg.solve_triangular(lower, sketch, lower=True) * (LEV * NX * NY) ** 0.5
    return (basis.reshape(probes.shape), core)
```

```python
import functools
import math

import jax
import jax.numpy as jnp
from jax import lax
from jax.experimental import pallas as pl
from jax.experimental.pallas import tpu as pltpu
from jax.sharding import PartitionSpec as P

MESH = pl.DeviceIdType.MESH
REACH = 4
WIND_REACH = REACH - 1
HIGHEST = lax.Precision.HIGHEST


def dot_t(x, y):
    return lax.dot_general(
        x, y, (((1,), (1,)), ((), ())), precision=HIGHEST, preferred_element_type=jnp.float32
    )


def sketch_kernel(
    n, ns, rows, scale,
    probes_ref, rec_ref, out_ref, core_ref,
    ext, recx, slots, first, second, third, total, sums_o, sums_s, parts,
    local_sem, zsend, zrecv, wsend, wrecv, osend, orecv, ssend, srecv, bsend, brecv,
):
    levels, count, columns = ext.shape[1:]
    share = rows // n
    each = count // n
    me = lax.axis_index("obs")
    here = lax.axis_index("space")
    base = me * share
    has_low = here > 0
    has_high = here < ns - 1

    barrier = pltpu.get_barrier_semaphore()
    for j in range(1, n):
        pl.semaphore_signal(
            barrier, inc=1, device_id={"obs": lax.rem(me + j, n)}, device_id_type=MESH
        )
    for j in range(1, ns):
        pl.semaphore_signal(
            barrier, inc=1, device_id={"space": lax.rem(here + j, ns)}, device_id_type=MESH
        )
    load_rec = pltpu.make_async_copy(rec_ref, recx.at[pl.ds(WIND_REACH, rows)], local_sem.at[0])
    load_probes = pltpu.make_async_copy(probes_ref, ext.at[pl.ds(REACH, rows)], local_sem.at[1])
    load_rec.start()
    load_probes.start()

    @pl.when(jnp.logical_not(has_low))
    def _():
        recx[pl.ds(0, WIND_REACH)] = jnp.zeros((WIND_REACH,) + recx.shape[1:], jnp.float32)
        for r in range(REACH):
            ext[r] = jnp.zeros(ext.shape[1:], jnp.float32)

    @pl.when(jnp.logical_not(has_high))
    def _():
        recx[pl.ds(WIND_REACH + rows, WIND_REACH)] = jnp.zeros(
            (WIND_REACH,) + recx.shape[1:], jnp.float32
        )
        for r in range(REACH):
            ext[REACH + rows + r] = jnp.zeros(ext.shape[1:], jnp.float32)

    pl.semaphore_wait(barrier, n - 1 + ns - 1)

    up = {"space": lax.rem(here + 1, ns)}
    down = {"space": lax.rem(here + ns - 1, ns)}
    need_low = base < REACH
    need_high = (n - 1 - me) * share < REACH

    def z_copy(index, source, target, device):
        return pltpu.make_async_remote_copy(
            src_ref=source, dst_ref=target, send_sem=zsend.at[index], recv_sem=zrecv.at[index],
            device_id=device, device_id_type=MESH,
        )

    rec_up = z_copy(
        0, rec_ref.at[pl.ds(rows - WIND_REACH, WIND_REACH)], recx.at[pl.ds(0, WIND_REACH)], up
    )
    probes_up = z_copy(1, probes_ref.at[pl.ds(rows - REACH, REACH)], ext.at[pl.ds(0, REACH)], up)
    rec_down = z_copy(
        2, rec_ref.at[pl.ds(0, WIND_REACH)], recx.at[pl.ds(WIND_REACH + rows, WIND_REACH)], down
    )
    probes_down = z_copy(
        3, probes_ref.at[pl.ds(0, REACH)], ext.at[pl.ds(REACH + rows, REACH)], down
    )
    sends_up = jnp.logical_and(has_high, need_low)
    sends_down = jnp.logical_and(has_low, need_high)
    pl.when(has_high)(rec_up.start)
    pl.when(has_low)(rec_down.start)
    pl.when(sends_up)(probes_up.start)
    pl.when(sends_down)(probes_down.start)

    load_rec.wait()
    pl.when(has_low)(rec_up.wait_recv)
    pl.when(has_high)(rec_down.wait_recv)

    span = share + 2 * WIND_REACH

    def other(j):
        if n & (n - 1):
            return lax.rem(me + j, n)
        peer, bit = me, 1
        while bit < n:
            if j & bit:
                peer = peer + bit * (1 - 2 * lax.rem(me // bit, 2))
            bit *= 2
        return peer

    def w_copy(j):
        peer = other(j)
        slot = j if not n & (n - 1) else n - j
        return pltpu.make_async_remote_copy(
            src_ref=recx.at[pl.ds(peer * share, span)], dst_ref=slots.at[slot],
            send_sem=wsend.at[j], recv_sem=wrecv.at[slot],
            device_id={"obs": peer}, device_id_type=MESH,
        )

    own = pltpu.make_async_copy(recx.at[pl.ds(base, span)], slots.at[0], local_sem.at[2])
    own.start()
    winds = [w_copy(j) for j in range(1, n)]
    for copy in winds:
        copy.start()
    total[...] = jnp.zeros_like(total)
    own.wait()
    load_probes.wait()
    pl.when(jnp.logical_and(has_low, need_low))(probes_up.wait_recv)
    pl.when(jnp.logical_and(has_high, need_high))(probes_down.wait_recv)

    column = lax.broadcasted_iota(jnp.int32, (levels, columns), 1)
    inside_right = column < columns - 1
    inside_left = column > 0

    def valid(row):
        at = here * rows + row
        return jnp.where(jnp.logical_and(at >= 0, at < ns * rows), 1.0, 0.0).astype(jnp.float32)

    def wind_of(j, row, which):
        return slots[j, row, pl.ds(which * 8, 8), :][:levels]

    def advance(upper, centre, lower, cu, cd, cr, cl, keep, finish):
        cr = jnp.where(inside_right, cr, 0.0) * keep
        cl = jnp.where(inside_left, cl, 0.0) * keep
        cu = cu * keep
        cd = cd * keep
        mid = 0.2 * keep
        vertical = 0.1 * keep
        for lev in range(levels):
            u = centre[lev]
            if levels == 1:
                beside = jnp.zeros_like(u)
            elif lev == 0:
                beside = centre[1]
            elif lev == levels - 1:
                beside = centre[lev - 1]
            else:
                beside = centre[lev - 1] + centre[lev + 1]
            value = (
                mid * u
                + vertical * beside
                + cu[lev : lev + 1] * upper[lev]
                + cd[lev : lev + 1] * lower[lev]
                + cr[lev : lev + 1] * pltpu.roll(u, columns - 1, 1)
                + cl[lev : lev + 1] * pltpu.roll(u, 1, 1)
            )
            finish(lev, value)

    def window(j, carry):
        @pl.when(j > 0)
        def _():
            pltpu.make_async_remote_copy(
                src_ref=recx.at[pl.ds(0, span)], dst_ref=slots.at[j],
                send_sem=wsend.at[j], recv_sem=wrecv.at[j],
                device_id={"obs": lax.rem(me + 1, n)}, device_id_type=MESH,
            ).wait_recv()

        def forward_1(k, c):
            at = base + k + 1
            a, b = 0.5 * wind_of(j, k, 0), 0.5 * wind_of(j, k, 1)

            def finish(lev, value):
                first[k, lev] = value

            advance(
                ext.at[at + 1], ext.at[at], ext.at[at - 1],
                0.15 - a, 0.15 + a, 0.15 - b, 0.15 + b, valid(base + k - 3), finish,
            )
            return c

        def forward_2(k, c):
            a, b = 0.5 * wind_of(j, k + 1, 2), 0.5 * wind_of(j, k + 1, 3)
            weight = wind_of(j, k + 1, 4)

            def finish(lev, value):
                second[k, lev] = value * weight[lev : lev + 1]

            advance(
                first.at[k + 2], first.at[k + 1], first.at[k],
                0.15 - a, 0.15 + a, 0.15 - b, 0.15 + b, jnp.float32(1.0), finish,
            )
            return c

        def across(b):
            return 0.15 + pltpu.roll(b, columns - 1, 1), 0.15 - pltpu.roll(b, 1, 1)

        def adjoint_1(k, c):
            cr, cl = across(0.5 * wind_of(j, k + 2, 3))

            def finish(lev, value):
                third[k, lev] = value

            advance(
                second.at[k + 2], second.at[k + 1], second.at[k],
                0.15 + 0.5 * wind_of(j, k + 3, 2), 0.15 - 0.5 * wind_of(j, k + 1, 2),
                cr, cl, valid(base + k - 1), finish,
            )
            return c

        def adjoint_2(k, c):
            cr, cl = across(0.5 * wind_of(j, k + 3, 1))

            def finish(lev, value):
                total[k, lev] += value

            advance(
                third.at[k + 2], third.at[k + 1], third.at[k],
                0.15 + 0.5 * wind_of(j, k + 4, 0), 0.15 - 0.5 * wind_of(j, k + 2, 0),
                cr, cl, jnp.float32(1.0), finish,
            )
            return c

        lax.fori_loop(0, share + 6, forward_1, 0)
        lax.fori_loop(0, share + 4, forward_2, 0)
        lax.fori_loop(0, share + 2, adjoint_1, 0)
        lax.fori_loop(0, share, adjoint_2, 0)
        return carry

    lax.fori_loop(0, n, window, 0)

    products = jnp.zeros((count, 2 * count), jnp.float32)
    for k in range(share):
        for lev in range(levels):
            s = total[k, lev]
            both = jnp.concatenate([ext[base + REACH + k, lev], s], axis=0)
            products = products + dot_t(s, both)

    half = count // 2

    def summed(buffer, axis, size, index, send, recv, value):
        buffer[index] = value
        copies = []
        for j in range(1, size):
            peer = lax.rem(index + j, size)
            copies.append(
                pltpu.make_async_remote_copy(
                    src_ref=buffer.at[index], dst_ref=buffer.at[index],
                    send_sem=send.at[j], recv_sem=recv.at[j],
                    device_id={axis: peer}, device_id_type=MESH,
                )
            )
            copies[-1].start()
        for copy in copies:
            copy.wait()
        result = buffer[0]
        for j in range(1, size):
            result = result + buffer[j]
        return result

    packed = jnp.concatenate([products[:half], products[half:]], axis=1)
    packed = summed(sums_o, "obs", n, me, osend, orecv, packed)
    packed = summed(sums_s, "space", ns, here, ssend, srecv, packed)
    products = jnp.concatenate([packed[:, : 2 * count], packed[:, 2 * count :]], axis=0)
    core_ref[...] = products

    row_id = lax.broadcasted_iota(jnp.int32, (count, 2 * count), 0)
    lane_id = lax.broadcasted_iota(jnp.int32, (count, 2 * count), 1)
    work = jnp.where(lane_id < count, jnp.where(lane_id == row_id, 1.0, 0.0), products)
    for k in range(count):
        pivot = work[k : k + 1, :]
        root = lax.rsqrt(work[k : k + 1, count + k : count + k + 1])
        pivot = pivot * root
        factor = work[:, count + k : count + k + 1] * root
        work = jnp.where(
            row_id > k, work - factor * pivot, jnp.where(row_id == k, pivot, work)
        )
    inverse = work[:, :count] * scale

    copies = []
    for k in range(share):
        for lev in range(levels):
            block = jnp.dot(
                inverse, total[k, lev], precision=HIGHEST, preferred_element_type=jnp.float32
            )
            for p in range(n):
                parts[p, k, lev] = block[p * each : (p + 1) * each]
        for j in range(1, n):
            peer = other(j)
            copy = pltpu.make_async_remote_copy(
                src_ref=parts.at[peer, k], dst_ref=out_ref.at[base + k],
                send_sem=bsend.at[k, j], recv_sem=brecv.at[k, j],
                device_id={"obs": peer}, device_id_type=MESH,
            )
            copy.start()
            copies.append(copy)
        out_ref[base + k] = parts[me, k]

    for copy in copies:
        copy.wait()
    for copy in winds:
        copy.wait_send()
    pl.when(has_high)(rec_up.wait_send)
    pl.when(has_low)(rec_down.wait_send)
    pl.when(sends_up)(probes_up.wait_send)
    pl.when(sends_down)(probes_down.wait_send)


def on_device(probes, wind, station_cell, obs_count, obs_weight):
    count, levels, rows, columns = probes.shape
    n = lax.axis_size("obs")
    ns = lax.axis_size("space")
    slots = station_cell.shape[1]
    share = rows // n
    each = count // n

    live = lax.iota(jnp.int32, slots) < obs_count[0, 0]
    weight = jnp.where(live, obs_weight[0], 0.0)
    cells = station_cell[0]
    at_row = lax.broadcasted_iota(jnp.int32, (levels * rows, slots), 0) == (cells // columns)[None]
    at_column = lax.broadcasted_iota(jnp.int32, (columns, slots), 0) == (cells % columns)[None]
    weights = dot_t(
        jnp.where(at_row, weight[None], 0.0), at_column.astype(jnp.float32)
    ).reshape(levels, rows, columns)

    fields = [wind[0, 0, 0], wind[0, 0, 1], wind[0, 1, 0], wind[0, 1, 1], weights]
    record = jnp.stack(fields)
    record = jnp.pad(record, [(0, 0), (0, 8 - levels), (0, 0), (0, 0)])
    record = record.transpose(2, 0, 1, 3).reshape(rows, 8 * len(fields), columns)
    probes_t = probes.transpose(2, 1, 0, 3)

    depth = record.shape[1]
    f32 = jnp.float32
    dma = pltpu.SemaphoreType.DMA
    out, products = pl.pallas_call(
        functools.partial(sketch_kernel, n, ns, rows, math.sqrt(levels * rows * ns * columns)),
        out_shape=(
            jax.ShapeDtypeStruct((rows, levels, each, columns), f32),
            jax.ShapeDtypeStruct((count, 2 * count), f32),
        ),
        in_specs=[pl.BlockSpec(memory_space=pl.ANY)] * 2,
        out_specs=(
            pl.BlockSpec(memory_space=pltpu.VMEM),
            pl.BlockSpec(memory_space=pltpu.VMEM),
        ),
        scratch_shapes=[
            pltpu.VMEM((rows + 2 * REACH, levels, count, columns), f32),
            pltpu.VMEM((rows + 2 * WIND_REACH, depth, columns), f32),
            pltpu.VMEM((n, share + 2 * WIND_REACH, depth, columns), f32),
            pltpu.VMEM((share + 6, levels, count, columns), f32),
            pltpu.VMEM((share + 4, levels, count, columns), f32),
            pltpu.VMEM((share + 2, levels, count, columns), f32),
            pltpu.VMEM((share, levels, count, columns), f32),
            pltpu.VMEM((n, count // 2, 4 * count), f32),
            pltpu.VMEM((ns, count // 2, 4 * count), f32),
            pltpu.VMEM((n, share, levels, each, columns), f32),
            dma((3,)), dma((4,)), dma((4,)), dma((n,)), dma((n,)),
            dma((n,)), dma((n,)), dma((ns,)), dma((ns,)), dma((share, n)), dma((share, n)),
        ],
        compiler_params=pltpu.CompilerParams(
            collective_id=0, has_side_effects=True, vmem_limit_bytes=40 * 2**20
        ),
    )(probes_t, record)
    basis = out.transpose(2, 1, 0, 3)
    core = products[:, :count].T / (n * ns * slots)
    return basis, core


def solution(mesh):
    in_specs = (
        P(None, None, "space", None),
        P("obs", None, None, None, "space", None),
        P("obs", "space"),
        P("obs", "space"),
        P("obs", "space"),
    )
    out_specs = (P("obs", None, "space", None), P())
    return jax.shard_map(
        on_device, mesh=mesh, in_specs=in_specs, out_specs=out_specs, check_vma=False
    )
```

```python
import functools
import math

import jax
import jax.numpy as jnp
from jax import lax
from jax.experimental import pallas as pl
from jax.experimental.pallas import tpu as pltpu
from jax.sharding import PartitionSpec as P

MESH = pl.DeviceIdType.MESH
REACH = 4
WIND_REACH = REACH - 1
HIGHEST = lax.Precision.HIGHEST


def dot_t(x, y):
    return lax.dot_general(
        x, y, (((1,), (1,)), ((), ())), precision=HIGHEST, preferred_element_type=jnp.float32
    )


def sketch_kernel(
    n, ns, rows, scale, divisor,
    probes_ref, wind_ref, cells_ref, live_ref, weight_ref, out_ref, core_ref,
    ext, recx, slots, first, second, third, total, sums_o, sums_s, parts,
    local_sem, zsend, zrecv, wsend, wrecv, osend, orecv, ssend, srecv, bsend, brecv,
):
    levels, count, columns = ext.shape[1:]
    share = rows // n
    each = count // n
    me = lax.axis_index("obs")
    here = lax.axis_index("space")
    base = me * share
    has_low = here > 0
    has_high = here < ns - 1

    barrier = pltpu.get_barrier_semaphore()
    for j in range(1, n):
        pl.semaphore_signal(
            barrier, inc=1, device_id={"obs": lax.rem(me + j, n)}, device_id_type=MESH
        )
    for j in range(1, ns):
        pl.semaphore_signal(
            barrier, inc=1, device_id={"space": lax.rem(here + j, ns)}, device_id_type=MESH
        )
    depth = wind_ref.shape[1]
    load_rec = pltpu.make_async_copy(
        wind_ref, recx.at[pl.ds(WIND_REACH, rows), pl.ds(0, depth)], local_sem.at[0]
    )
    load_probes = pltpu.make_async_copy(probes_ref, ext.at[pl.ds(REACH, rows)], local_sem.at[1])
    load_rec.start()
    load_probes.start()

    @pl.when(jnp.logical_not(has_low))
    def _():
        recx[pl.ds(0, WIND_REACH)] = jnp.zeros((WIND_REACH,) + recx.shape[1:], jnp.float32)
        for r in range(REACH):
            ext[r] = jnp.zeros(ext.shape[1:], jnp.float32)

    @pl.when(jnp.logical_not(has_high))
    def _():
        recx[pl.ds(WIND_REACH + rows, WIND_REACH)] = jnp.zeros(
            (WIND_REACH,) + recx.shape[1:], jnp.float32
        )
        for r in range(REACH):
            ext[REACH + rows + r] = jnp.zeros(ext.shape[1:], jnp.float32)

    cells = cells_ref[...]
    slot_count = cells.shape[1]
    slot = lax.broadcasted_iota(jnp.int32, (1, slot_count), 1)
    weight = jnp.where(slot < live_ref[0, 0], weight_ref[...], 0.0)
    line = lax.broadcasted_iota(jnp.int32, (rows * levels, slot_count), 0)
    start = (lax.rem(line, levels) * rows + lax.div(line, levels)) * columns
    on_line = jnp.logical_and(cells >= start, cells < start + columns)
    at_column = lax.rem(cells, columns) == lax.broadcasted_iota(
        jnp.int32, (columns, slot_count), 0
    )
    weights = dot_t(
        jnp.where(on_line, weight, 0.0), jnp.where(at_column, 1.0, 0.0).astype(jnp.float32)
    )
    for r in range(rows):
        recx[WIND_REACH + r, pl.ds(depth, levels)] = weights[r * levels : (r + 1) * levels]
    total[...] = jnp.zeros_like(total)
    load_rec.wait()

    pl.semaphore_wait(barrier, n - 1 + ns - 1)

    up = {"space": lax.rem(here + 1, ns)}
    down = {"space": lax.rem(here + ns - 1, ns)}
    need_low = base < REACH
    need_high = (n - 1 - me) * share < REACH

    def z_copy(index, source, target, device):
        return pltpu.make_async_remote_copy(
            src_ref=source, dst_ref=target, send_sem=zsend.at[index], recv_sem=zrecv.at[index],
            device_id=device, device_id_type=MESH,
        )

    rec_up = z_copy(
        0, recx.at[pl.ds(rows, WIND_REACH)], recx.at[pl.ds(0, WIND_REACH)], up
    )
    rec_down = z_copy(
        1, recx.at[pl.ds(WIND_REACH, WIND_REACH)],
        recx.at[pl.ds(WIND_REACH + rows, WIND_REACH)], down,
    )
    probes_up = [
        z_copy(2 + h, probes_ref.at[rows - REACH + h], ext.at[h], up) for h in range(REACH)
    ]
    probes_down = [
        z_copy(2 + REACH + h, probes_ref.at[h], ext.at[REACH + rows + h], down)
        for h in range(REACH)
    ]
    sends_up = jnp.logical_and(has_high, need_low)
    sends_down = jnp.logical_and(has_low, need_high)
    pl.when(has_high)(rec_up.start)
    pl.when(has_low)(rec_down.start)
    for copy in reversed(probes_up):
        pl.when(sends_up)(copy.start)
    for copy in probes_down:
        pl.when(sends_down)(copy.start)
    pl.when(has_low)(rec_up.wait_recv)
    pl.when(has_high)(rec_down.wait_recv)

    span = share + 2 * WIND_REACH

    def other(j):
        if n & (n - 1):
            return lax.rem(me + j, n)
        peer, bit = me, 1
        while bit < n:
            if j & bit:
                peer = peer + bit * (1 - 2 * lax.rem(me // bit, 2))
            bit *= 2
        return peer

    def w_copy(j):
        peer = other(j)
        slot = j if not n & (n - 1) else n - j
        return pltpu.make_async_remote_copy(
            src_ref=recx.at[pl.ds(peer * share, span)], dst_ref=slots.at[slot],
            send_sem=wsend.at[j], recv_sem=wrecv.at[slot],
            device_id={"obs": peer}, device_id_type=MESH,
        )

    own = pltpu.make_async_copy(recx.at[pl.ds(base, span)], slots.at[0], local_sem.at[2])
    own.start()
    winds = [w_copy(j) for j in range(1, n)]
    for copy in winds:
        copy.start()
    own.wait()
    load_probes.wait()
    gets_low = jnp.logical_and(has_low, need_low)
    gets_high = jnp.logical_and(has_high, need_high)

    column = lax.broadcasted_iota(jnp.int32, (levels, columns), 1)
    inside_right = column < columns - 1
    inside_left = column > 0

    def valid(row):
        at = here * rows + row
        return jnp.where(jnp.logical_and(at >= 0, at < ns * rows), 1.0, 0.0).astype(jnp.float32)

    def wind_of(j, row, which):
        return slots[j, row, pl.ds(which * levels, levels), :]

    def advance(upper, centre, lower, cu, cd, cr, cl, keep, finish):
        cr = jnp.where(inside_right, cr, 0.0) * keep
        cl = jnp.where(inside_left, cl, 0.0) * keep
        cu = cu * keep
        cd = cd * keep
        mid = 0.2 * keep
        vertical = 0.1 * keep
        for lev in range(levels):
            u = centre[lev]
            if levels == 1:
                beside = jnp.zeros_like(u)
            elif lev == 0:
                beside = centre[1]
            elif lev == levels - 1:
                beside = centre[lev - 1]
            else:
                beside = centre[lev - 1] + centre[lev + 1]
            value = (
                mid * u
                + vertical * beside
                + cu[lev : lev + 1] * upper[lev]
                + cd[lev : lev + 1] * lower[lev]
                + cr[lev : lev + 1] * pltpu.roll(u, columns - 1, 1)
                + cl[lev : lev + 1] * pltpu.roll(u, 1, 1)
            )
            finish(lev, value)

    def forward_1(j, k):
        at = base + k + 1
        a, b = 0.5 * wind_of(j, k, 0), 0.5 * wind_of(j, k, 1)

        def finish(lev, value):
            first[k, lev] = value

        advance(
            ext.at[at + 1], ext.at[at], ext.at[at - 1],
            0.15 - a, 0.15 + a, 0.15 - b, 0.15 + b, valid(base + k - 3), finish,
        )

    both_sides = jnp.logical_and(need_low, need_high)
    for h in range(REACH):
        pl.when(jnp.logical_and(gets_high, both_sides))(probes_down[h].wait_recv)

    def arriving(i, c):
        k = jnp.where(need_low, span - 1 - i, i)
        for h in range(REACH):
            pl.when(jnp.logical_and(gets_low, base + k == h))(probes_up[h].wait_recv)
            pl.when(
                jnp.logical_and(
                    jnp.logical_and(gets_high, jnp.logical_not(both_sides)),
                    base + k + 2 == REACH + rows + h,
                )
            )(probes_down[h].wait_recv)
        forward_1(0, k)
        return c

    lax.fori_loop(0, span, arriving, 0)
    for h in range(REACH):
        pl.when(jnp.logical_and(gets_low, h < base))(probes_up[h].wait_recv)
        pl.when(
            jnp.logical_and(
                jnp.logical_and(gets_high, jnp.logical_not(both_sides)),
                base + span + 1 < REACH + rows + h,
            )
        )(probes_down[h].wait_recv)

    def window(j, carry):
        @pl.when(j > 0)
        def _():
            pltpu.make_async_remote_copy(
                src_ref=recx.at[pl.ds(0, span)], dst_ref=slots.at[j],
                send_sem=wsend.at[j], recv_sem=wrecv.at[j],
                device_id={"obs": lax.rem(me + 1, n)}, device_id_type=MESH,
            ).wait_recv()

            def step(k, c):
                forward_1(j, k)
                return c

            lax.fori_loop(0, span, step, 0, unroll=2 if span % 2 == 0 else 1)

        def forward_2(k, c):
            a, b = 0.5 * wind_of(j, k + 1, 2), 0.5 * wind_of(j, k + 1, 3)
            weight = wind_of(j, k + 1, 4)

            def finish(lev, value):
                second[k, lev] = value * weight[lev : lev + 1]

            advance(
                first.at[k + 2], first.at[k + 1], first.at[k],
                0.15 - a, 0.15 + a, 0.15 - b, 0.15 + b, jnp.float32(1.0), finish,
            )
            return c

        def across(b):
            return 0.15 + pltpu.roll(b, columns - 1, 1), 0.15 - pltpu.roll(b, 1, 1)

        def adjoint_1(k, c):
            cr, cl = across(0.5 * wind_of(j, k + 2, 3))

            def finish(lev, value):
                third[k, lev] = value

            advance(
                second.at[k + 2], second.at[k + 1], second.at[k],
                0.15 + 0.5 * wind_of(j, k + 3, 2), 0.15 - 0.5 * wind_of(j, k + 1, 2),
                cr, cl, valid(base + k - 1), finish,
            )
            return c

        def adjoint_2(k, c):
            cr, cl = across(0.5 * wind_of(j, k + 3, 1))

            def finish(lev, value):
                total[k, lev] += value

            advance(
                third.at[k + 2], third.at[k + 1], third.at[k],
                0.15 + 0.5 * wind_of(j, k + 4, 0), 0.15 - 0.5 * wind_of(j, k + 2, 0),
                cr, cl, jnp.float32(1.0), finish,
            )
            return c

        unroll = 2 if share % 2 == 0 else 1
        lax.fori_loop(0, share + 4, forward_2, 0, unroll=unroll)
        lax.fori_loop(0, share + 2, adjoint_1, 0, unroll=unroll)
        lax.fori_loop(0, share, adjoint_2, 0, unroll=unroll)
        return carry

    lax.fori_loop(0, n, window, 0)

    products = jnp.zeros((2 * count, count), jnp.float32)
    for k in range(share):
        for lev in range(levels):
            s = total[k, lev]
            both = jnp.concatenate([ext[base + REACH + k, lev], s], axis=0)
            products = products + dot_t(both, s)

    half = count // 2

    def summed(buffer, axis, size, index, send, recv, value):
        buffer[index] = value
        copies = []
        for j in range(1, size):
            peer = lax.rem(index + j, size)
            copies.append(
                pltpu.make_async_remote_copy(
                    src_ref=buffer.at[index], dst_ref=buffer.at[index],
                    send_sem=send.at[j], recv_sem=recv.at[j],
                    device_id={axis: peer}, device_id_type=MESH,
                )
            )
            copies[-1].start()
        for copy in copies:
            copy.wait()
        result = buffer[0]
        for j in range(1, size):
            result = result + buffer[j]
        return result

    packed = jnp.concatenate(
        [products[i * half : (i + 1) * half] for i in (0, 2, 1, 3)], axis=1
    )
    packed = summed(sums_o, "obs", n, me, osend, orecv, packed)
    packed = summed(sums_s, "space", ns, here, ssend, srecv, packed)
    products = jnp.concatenate([packed[:, : 2 * count], packed[:, 2 * count :]], axis=0)
    core_ref[...] = products[:, :count] * (1.0 / divisor)

    row_id = lax.broadcasted_iota(jnp.int32, (count, 2 * count), 0)
    lane_id = lax.broadcasted_iota(jnp.int32, (count, 2 * count), 1)
    work = jnp.where(lane_id < count, jnp.where(lane_id == row_id, 1.0, 0.0), products)
    for k in range(count - 1):
        pivot = work[k : k + 1, :]
        inverse = 1.0 / work[k : k + 1, count + k : count + k + 1]
        factor = jnp.where(row_id > k, work[:, count + k : count + k + 1], 0.0)
        work = work - (factor * pivot) * inverse
    diagonal = jnp.sum(jnp.where(lane_id == row_id + count, work, 0.0), axis=1, keepdims=True)
    inverse = work[:, :count] * (lax.rsqrt(diagonal) * scale)

    copies = []
    for k in range(share):
        for lev in range(levels):
            block = jnp.dot(
                inverse, total[k, lev], precision=HIGHEST, preferred_element_type=jnp.float32
            )
            for p in range(n):
                parts[p, k, lev] = block[p * each : (p + 1) * each]
        for j in range(1, n):
            peer = other(j)
            copy = pltpu.make_async_remote_copy(
                src_ref=parts.at[peer, k], dst_ref=out_ref.at[base + k],
                send_sem=bsend.at[k, j], recv_sem=brecv.at[k, j],
                device_id={"obs": peer}, device_id_type=MESH,
            )
            copy.start()
            copies.append(copy)
        out_ref[base + k] = parts[me, k]

    for copy in copies:
        copy.wait()
    for copy in winds:
        copy.wait_send()
    pl.when(has_high)(rec_up.wait_send)
    pl.when(has_low)(rec_down.wait_send)
    for copy in probes_up:
        pl.when(sends_up)(copy.wait_send)
    for copy in probes_down:
        pl.when(sends_down)(copy.wait_send)


def on_device(probes, wind, station_cell, obs_count, obs_weight):
    count, levels, rows, columns = probes.shape
    n = lax.axis_size("obs")
    ns = lax.axis_size("space")
    slots = station_cell.shape[1]
    share = rows // n
    each = count // n

    steps, components = wind.shape[1:3]
    lines = steps * components * levels
    wind_t = wind[0].transpose(3, 0, 1, 2, 4).reshape(rows, lines, columns)
    probes_t = probes.transpose(2, 1, 0, 3)
    depth = lines + 8 * pl.cdiv(levels, 8)

    f32 = jnp.float32
    dma = pltpu.SemaphoreType.DMA
    out, core = pl.pallas_call(
        functools.partial(
            sketch_kernel, n, ns, rows, math.sqrt(levels * rows * ns * columns), n * ns * slots
        ),
        out_shape=(
            jax.ShapeDtypeStruct((rows, levels, each, columns), f32),
            jax.ShapeDtypeStruct((count, count), f32),
        ),
        in_specs=[
            pl.BlockSpec(memory_space=pl.ANY),
            pl.BlockSpec(memory_space=pl.ANY),
            pl.BlockSpec(memory_space=pltpu.VMEM),
            pl.BlockSpec(memory_space=pltpu.SMEM),
            pl.BlockSpec(memory_space=pltpu.VMEM),
        ],
        out_specs=(
            pl.BlockSpec(memory_space=pltpu.VMEM),
            pl.BlockSpec(memory_space=pltpu.VMEM),
        ),
        scratch_shapes=[
            pltpu.VMEM((rows + 2 * REACH, levels, count, columns), f32),
            pltpu.VMEM((rows + 2 * WIND_REACH, depth, columns), f32),
            pltpu.VMEM((n, share + 2 * WIND_REACH, depth, columns), f32),
            pltpu.VMEM((share + 6, levels, count, columns), f32),
            pltpu.VMEM((share + 4, levels, count, columns), f32),
            pltpu.VMEM((share + 2, levels, count, columns), f32),
            pltpu.VMEM((share, levels, count, columns), f32),
            pltpu.VMEM((n, count // 2, 4 * count), f32),
            pltpu.VMEM((ns, count // 2, 4 * count), f32),
            pltpu.VMEM((n, share, levels, each, columns), f32),
            dma((3,)), dma((2 + 2 * REACH,)), dma((2 + 2 * REACH,)), dma((n,)), dma((n,)),
            dma((n,)), dma((n,)), dma((ns,)), dma((ns,)), dma((share, n)), dma((share, n)),
        ],
        compiler_params=pltpu.CompilerParams(
            collective_id=0, has_side_effects=True, vmem_limit_bytes=40 * 2**20
        ),
    )(probes_t, wind_t, station_cell, obs_count, obs_weight)
    basis = out.transpose(2, 1, 0, 3)
    return basis, core


def solution(mesh):
    in_specs = (
        P(None, None, "space", None),
        P("obs", None, None, None, "space", None),
        P("obs", "space"),
        P("obs", "space"),
        P("obs", "space"),
    )
    out_specs = (P("obs", None, "space", None), P())
    return jax.shard_map(
        on_device, mesh=mesh, in_specs=in_specs, out_specs=out_specs, check_vma=False
    )
```

```python
import functools
import math

import jax
import jax.numpy as jnp
from jax import lax
from jax.experimental import pallas as pl
from jax.experimental.pallas import tpu as pltpu
from jax.sharding import PartitionSpec as P

MESH = pl.DeviceIdType.MESH
REACH = 4
WIND_REACH = REACH - 1
HIGHEST = lax.Precision.HIGHEST


def dot_t(x, y):
    return lax.dot_general(
        x, y, (((1,), (1,)), ((), ())), precision=HIGHEST, preferred_element_type=jnp.float32
    )


def sketch_kernel(
    n, ns, rows, scale, divisor,
    probes_ref, wind_ref, cells_ref, live_ref, weight_ref, out_ref, core_ref,
    ext, recx, slots, first, second, third, total, sums_o, sums_s, parts,
    wind_raw, probes_raw, local_sem, zsend, zrecv, wsend, wrecv, osend, orecv, ssend, srecv, bsend, brecv,
):
    levels, count, columns = ext.shape[1:]
    share = rows // n
    each = count // n
    me = lax.axis_index("obs")
    here = lax.axis_index("space")
    base = me * share
    has_low = here > 0
    has_high = here < ns - 1

    barrier = pltpu.get_barrier_semaphore()
    for j in range(1, n):
        pl.semaphore_signal(
            barrier, inc=1, device_id={"obs": lax.rem(me + j, n)}, device_id_type=MESH
        )
    for j in range(1, ns):
        pl.semaphore_signal(
            barrier, inc=1, device_id={"space": lax.rem(here + j, ns)}, device_id_type=MESH
        )
    depth = wind_ref.shape[0]
    need_low = base < REACH
    need_high = (n - 1 - me) * share < REACH
    load_winds = pltpu.make_async_copy(wind_ref, wind_raw, local_sem.at[0])
    load_probes = pltpu.make_async_copy(probes_ref, probes_raw, local_sem.at[1])
    load_winds.start()
    load_probes.start()

    @pl.when(jnp.logical_not(has_low))
    def _():
        recx[pl.ds(0, WIND_REACH)] = jnp.zeros((WIND_REACH,) + recx.shape[1:], jnp.float32)
        for r in range(REACH):
            ext[r] = jnp.zeros(ext.shape[1:], jnp.float32)

    @pl.when(jnp.logical_not(has_high))
    def _():
        recx[pl.ds(WIND_REACH + rows, WIND_REACH)] = jnp.zeros(
            (WIND_REACH,) + recx.shape[1:], jnp.float32
        )
        for r in range(REACH):
            ext[REACH + rows + r] = jnp.zeros(ext.shape[1:], jnp.float32)

    cells = cells_ref[...]
    slot_count = cells.shape[1]
    slot = lax.broadcasted_iota(jnp.int32, (1, slot_count), 1)
    weight = jnp.where(slot < live_ref[0, 0], weight_ref[...], 0.0)
    line = lax.broadcasted_iota(jnp.int32, (rows * levels, slot_count), 0)
    start = (lax.rem(line, levels) * rows + lax.div(line, levels)) * columns
    on_line = jnp.logical_and(cells >= start, cells < start + columns)
    at_column = lax.rem(cells, columns) == lax.broadcasted_iota(
        jnp.int32, (columns, slot_count), 0
    )
    weights = dot_t(
        jnp.where(on_line, weight, 0.0), jnp.where(at_column, 1.0, 0.0).astype(jnp.float32)
    )
    for r in range(rows):
        recx[WIND_REACH + r, pl.ds(depth, levels)] = weights[r * levels : (r + 1) * levels]
    total[...] = jnp.zeros_like(total)
    load_winds.wait()
    recx[pl.ds(WIND_REACH, rows), pl.ds(0, depth)] = jnp.swapaxes(wind_raw[...], 0, 1)

    pl.semaphore_wait(barrier, n - 1 + ns - 1)

    up = {"space": lax.rem(here + 1, ns)}
    down = {"space": lax.rem(here + ns - 1, ns)}

    def z_copy(index, source, target, device):
        return pltpu.make_async_remote_copy(
            src_ref=source, dst_ref=target, send_sem=zsend.at[index], recv_sem=zrecv.at[index],
            device_id=device, device_id_type=MESH,
        )

    rec_up = z_copy(
        0, recx.at[pl.ds(rows, WIND_REACH)], recx.at[pl.ds(0, WIND_REACH)], up
    )
    rec_down = z_copy(
        1, recx.at[pl.ds(WIND_REACH, WIND_REACH)],
        recx.at[pl.ds(WIND_REACH + rows, WIND_REACH)], down,
    )
    probes_up = [
        z_copy(2 + h, ext.at[rows + h], ext.at[h], up) for h in range(REACH)
    ]
    probes_down = [
        z_copy(2 + REACH + h, ext.at[REACH + h], ext.at[REACH + rows + h], down)
        for h in range(REACH)
    ]
    sends_up = jnp.logical_and(has_high, need_low)
    sends_down = jnp.logical_and(has_low, need_high)
    pl.when(has_high)(rec_up.start)
    pl.when(has_low)(rec_down.start)
    load_probes.wait()
    for lev in range(levels):
        ext[pl.ds(REACH, rows), lev] = jnp.swapaxes(probes_raw[:, lev], 0, 1)
    for copy in reversed(probes_up):
        pl.when(sends_up)(copy.start)
    for copy in probes_down:
        pl.when(sends_down)(copy.start)

    span = share + 2 * WIND_REACH

    def other(j):
        if n & (n - 1):
            return lax.rem(me + j, n)
        peer, bit = me, 1
        while bit < n:
            if j & bit:
                peer = peer + bit * (1 - 2 * lax.rem(me // bit, 2))
            bit *= 2
        return peer

    def w_copy(j):
        peer = other(j)
        slot = j if not n & (n - 1) else n - j
        return pltpu.make_async_remote_copy(
            src_ref=recx.at[pl.ds(peer * share, span)], dst_ref=slots.at[slot],
            send_sem=wsend.at[j], recv_sem=wrecv.at[slot],
            device_id={"obs": peer}, device_id_type=MESH,
        )

    gets_low = jnp.logical_and(has_low, need_low)
    gets_high = jnp.logical_and(has_high, need_high)

    column = lax.broadcasted_iota(jnp.int32, (levels, columns), 1)
    inside_right = column < columns - 1
    inside_left = column > 0

    def valid(row):
        at = here * rows + row
        return jnp.where(jnp.logical_and(at >= 0, at < ns * rows), 1.0, 0.0).astype(jnp.float32)

    def own_wind(row, which):
        return recx[base + row, pl.ds(which * levels, levels), :]

    def wind_in(j):
        return lambda row, which: slots[j, row, pl.ds(which * levels, levels), :]

    def advance(upper, centre, lower, cu, cd, cr, cl, keep, finish):
        cr = jnp.where(inside_right, cr, 0.0) * keep
        cl = jnp.where(inside_left, cl, 0.0) * keep
        cu = cu * keep
        cd = cd * keep
        mid = 0.2 * keep
        vertical = 0.1 * keep
        for lev in range(levels):
            u = centre[lev]
            if levels == 1:
                beside = jnp.zeros_like(u)
            elif lev == 0:
                beside = centre[1]
            elif lev == levels - 1:
                beside = centre[lev - 1]
            else:
                beside = centre[lev - 1] + centre[lev + 1]
            value = (
                mid * u
                + vertical * beside
                + cu[lev : lev + 1] * upper[lev]
                + cd[lev : lev + 1] * lower[lev]
                + cr[lev : lev + 1] * pltpu.roll(u, columns - 1, 1)
                + cl[lev : lev + 1] * pltpu.roll(u, 1, 1)
            )
            finish(lev, value)

    def forward_1(wind_of, k):
        at = base + k + 1
        a, b = 0.5 * wind_of(k, 0), 0.5 * wind_of(k, 1)

        def finish(lev, value):
            first[k, lev] = value

        advance(
            ext.at[at + 1], ext.at[at], ext.at[at - 1],
            0.15 - a, 0.15 + a, 0.15 - b, 0.15 + b, valid(base + k - 3), finish,
        )

    def forward_2(wind_of, k):
        a, b = 0.5 * wind_of(k + 1, 2), 0.5 * wind_of(k + 1, 3)
        weight = wind_of(k + 1, 4)

        def finish(lev, value):
            second[k, lev] = value * weight[lev : lev + 1]

        advance(
            first.at[k + 2], first.at[k + 1], first.at[k],
            0.15 - a, 0.15 + a, 0.15 - b, 0.15 + b, jnp.float32(1.0), finish,
        )

    def across(b):
        return 0.15 + pltpu.roll(b, columns - 1, 1), 0.15 - pltpu.roll(b, 1, 1)

    def adjoint_1(wind_of, k):
        cr, cl = across(0.5 * wind_of(k + 2, 3))

        def finish(lev, value):
            third[k, lev] = value

        advance(
            second.at[k + 2], second.at[k + 1], second.at[k],
            0.15 + 0.5 * wind_of(k + 3, 2), 0.15 - 0.5 * wind_of(k + 1, 2),
            cr, cl, valid(base + k - 1), finish,
        )

    def adjoint_2(wind_of, k):
        cr, cl = across(0.5 * wind_of(k + 3, 1))

        def finish(lev, value):
            total[k, lev] += value

        advance(
            third.at[k + 2], third.at[k + 1], third.at[k],
            0.15 + 0.5 * wind_of(k + 4, 0), 0.15 - 0.5 * wind_of(k + 2, 0),
            cr, cl, jnp.float32(1.0), finish,
        )

    both_sides = jnp.logical_and(need_low, need_high)
    ready = span
    for at in (p * share for p in range(n)):
        if at < REACH:
            ready = min(ready, span - (REACH - at))
        if (n - 1) * share - at < REACH:
            ready = min(ready, REACH + rows - 2 - at)
    wavefront = ready >= 6

    def place(i, stage):
        return jnp.where(need_low, span - 1 - i, i - 2 * stage)

    unroll = 2 if share % 2 == 0 else 1
    later = ((2, forward_2), (4, adjoint_1), (6, adjoint_2))

    def local_row(i, c):
        forward_1(own_wind, place(i, 0))
        return c

    def later_sweeps(end):
        for begin, step in later:

            def body(i, c):
                step(own_wind, place(i, begin // 2))
                return c

            if begin < end:
                lax.fori_loop(begin, end, body, 0, unroll=unroll)

    def arriving(i, c):
        k = place(i, 0)
        for h in range(REACH):
            pl.when(jnp.logical_and(gets_low, base + k == h))(probes_up[h].wait_recv)
            pl.when(
                jnp.logical_and(
                    jnp.logical_and(gets_high, jnp.logical_not(both_sides)),
                    base + k + 2 == REACH + rows + h,
                )
            )(probes_down[h].wait_recv)
        forward_1(own_wind, k)
        if wavefront:
            for begin, step in later:
                step(own_wind, place(i, begin // 2))
        return c

    if wavefront:
        lax.fori_loop(0, ready, local_row, 0, unroll=unroll)

    pl.when(has_low)(rec_up.wait_recv)
    pl.when(has_high)(rec_down.wait_recv)
    winds = [w_copy(j) for j in range(1, n)]
    for copy in winds:
        copy.start()

    if wavefront:
        later_sweeps(ready)
    for h in range(REACH):
        pl.when(jnp.logical_and(gets_high, both_sides))(probes_down[h].wait_recv)
    lax.fori_loop(ready if wavefront else 0, span, arriving, 0)
    for h in range(REACH):
        pl.when(jnp.logical_and(gets_low, h < base))(probes_up[h].wait_recv)
        pl.when(
            jnp.logical_and(
                jnp.logical_and(gets_high, jnp.logical_not(both_sides)),
                base + span + 1 < REACH + rows + h,
            )
        )(probes_down[h].wait_recv)

    if not wavefront:
        later_sweeps(span)

    def window(j, carry):
        pltpu.make_async_remote_copy(
            src_ref=recx.at[pl.ds(0, span)], dst_ref=slots.at[j],
            send_sem=wsend.at[j], recv_sem=wrecv.at[j],
            device_id={"obs": lax.rem(me + 1, n)}, device_id_type=MESH,
        ).wait_recv()

        def sweep(step, length):
            def body(k, c):
                step(wind_in(j), k)
                return c

            lax.fori_loop(0, length, body, 0, unroll=unroll)

        sweep(forward_1, share + 6)
        sweep(forward_2, share + 4)
        sweep(adjoint_1, share + 2)
        sweep(adjoint_2, share)
        return carry

    lax.fori_loop(1, n, window, 0)

    products = jnp.zeros((2 * count, count), jnp.float32)
    for k in range(share):
        for lev in range(levels):
            s = total[k, lev]
            both = jnp.concatenate([ext[base + REACH + k, lev], s], axis=0)
            products = products + dot_t(both, s)

    half = count // 2

    def summed(buffer, axis, size, index, send, recv, value):
        buffer[index] = value
        copies = []
        for j in range(1, size):
            peer = lax.rem(index + j, size)
            copies.append(
                pltpu.make_async_remote_copy(
                    src_ref=buffer.at[index], dst_ref=buffer.at[index],
                    send_sem=send.at[j], recv_sem=recv.at[j],
                    device_id={axis: peer}, device_id_type=MESH,
                )
            )
            copies[-1].start()
        for copy in copies:
            copy.wait()
        result = buffer[0]
        for j in range(1, size):
            result = result + buffer[j]
        return result

    packed = jnp.concatenate(
        [products[i * half : (i + 1) * half] for i in (0, 2, 1, 3)], axis=1
    )
    packed = summed(sums_o, "obs", n, me, osend, orecv, packed)
    packed = summed(sums_s, "space", ns, here, ssend, srecv, packed)
    products = jnp.concatenate([packed[:, : 2 * count], packed[:, 2 * count :]], axis=0)
    core_ref[...] = products[:, :count] * (1.0 / divisor)

    row_id = lax.broadcasted_iota(jnp.int32, (count, 2 * count), 0)
    lane_id = lax.broadcasted_iota(jnp.int32, (count, 2 * count), 1)
    work = jnp.where(lane_id < count, jnp.where(lane_id == row_id, 1.0, 0.0), products)
    for k in range(count - 1):
        pivot = work[k : k + 1, :]
        inverse = 1.0 / work[k : k + 1, count + k : count + k + 1]
        factor = jnp.where(row_id > k, work[:, count + k : count + k + 1], 0.0)
        work = work - (factor * pivot) * inverse
    diagonal = jnp.sum(jnp.where(lane_id == row_id + count, work, 0.0), axis=1, keepdims=True)
    inverse = work[:, :count] * (lax.rsqrt(diagonal) * scale)

    copies = []
    for k in range(share):
        for lev in range(levels):
            block = jnp.dot(
                inverse, total[k, lev], precision=HIGHEST, preferred_element_type=jnp.float32
            )
            for p in range(n):
                parts[p, k, lev] = block[p * each : (p + 1) * each]
        for j in range(1, n):
            peer = other(j)
            copy = pltpu.make_async_remote_copy(
                src_ref=parts.at[peer, k], dst_ref=out_ref.at[base + k],
                send_sem=bsend.at[k, j], recv_sem=brecv.at[k, j],
                device_id={"obs": peer}, device_id_type=MESH,
            )
            copy.start()
            copies.append(copy)
        out_ref[base + k] = parts[me, k]

    for copy in copies:
        copy.wait()
    for copy in winds:
        copy.wait_send()
    pl.when(has_high)(rec_up.wait_send)
    pl.when(has_low)(rec_down.wait_send)
    for copy in probes_up:
        pl.when(sends_up)(copy.wait_send)
    for copy in probes_down:
        pl.when(sends_down)(copy.wait_send)


def on_device(probes, wind, station_cell, obs_count, obs_weight):
    count, levels, rows, columns = probes.shape
    n = lax.axis_size("obs")
    ns = lax.axis_size("space")
    slots = station_cell.shape[1]
    share = rows // n
    each = count // n

    steps, components = wind.shape[1:3]
    lines = steps * components * levels
    winds = wind.reshape(lines, rows, columns)
    depth = lines + 8 * pl.cdiv(levels, 8)

    f32 = jnp.float32
    dma = pltpu.SemaphoreType.DMA
    out, core = pl.pallas_call(
        functools.partial(
            sketch_kernel, n, ns, rows, math.sqrt(levels * rows * ns * columns), n * ns * slots
        ),
        out_shape=(
            jax.ShapeDtypeStruct((rows, levels, each, columns), f32),
            jax.ShapeDtypeStruct((count, count), f32),
        ),
        in_specs=[
            pl.BlockSpec(memory_space=pltpu.HBM),
            pl.BlockSpec(memory_space=pltpu.HBM),
            pl.BlockSpec(memory_space=pltpu.VMEM),
            pl.BlockSpec(memory_space=pltpu.SMEM),
            pl.BlockSpec(memory_space=pltpu.VMEM),
        ],
        out_specs=(
            pl.BlockSpec(memory_space=pltpu.VMEM),
            pl.BlockSpec(memory_space=pltpu.VMEM),
        ),
        scratch_shapes=[
            pltpu.VMEM((rows + 2 * REACH, levels, count, columns), f32),
            pltpu.VMEM((rows + 2 * WIND_REACH, depth, columns), f32),
            pltpu.VMEM((n, share + 2 * WIND_REACH, depth, columns), f32),
            pltpu.VMEM((share + 6, levels, count, columns), f32),
            pltpu.VMEM((share + 4, levels, count, columns), f32),
            pltpu.VMEM((share + 2, levels, count, columns), f32),
            pltpu.VMEM((share, levels, count, columns), f32),
            pltpu.VMEM((n, count // 2, 4 * count), f32),
            pltpu.VMEM((ns, count // 2, 4 * count), f32),
            pltpu.VMEM((n, share, levels, each, columns), f32),
            pltpu.VMEM((lines, rows, columns), f32),
            pltpu.VMEM((count, levels, rows, columns), f32),
            dma((2,)), dma((2 + 2 * REACH,)), dma((2 + 2 * REACH,)), dma((n,)), dma((n,)),
            dma((n,)), dma((n,)), dma((ns,)), dma((ns,)), dma((share, n)), dma((share, n)),
        ],
        compiler_params=pltpu.CompilerParams(
            collective_id=0, has_side_effects=True, vmem_limit_bytes=40 * 2**20
        ),
    )(probes, winds, station_cell, obs_count, obs_weight)
    basis = out.transpose(2, 1, 0, 3)
    return basis, core


def solution(mesh):
    in_specs = (
        P(None, None, "space", None),
        P("obs", None, None, None, "space", None),
        P("obs", "space"),
        P("obs", "space"),
        P("obs", "space"),
    )
    out_specs = (P("obs", None, "space", None), P())
    return jax.shard_map(
        on_device, mesh=mesh, in_specs=in_specs, out_specs=out_specs, check_vma=False
    )
```

```python
import functools
import math

import jax
import jax.numpy as jnp
from jax import lax
from jax.experimental import pallas as pl
from jax.experimental.pallas import tpu as pltpu
from jax.sharding import PartitionSpec as P

MESH = pl.DeviceIdType.MESH
REACH = 4
WIND_REACH = REACH - 1
VMEM_BYTES = 64 * 2**20
HIGHEST = lax.Precision.HIGHEST


def dot_t(x, y):
    return lax.dot_general(
        x, y, (((1,), (1,)), ((), ())), precision=HIGHEST, preferred_element_type=jnp.float32
    )


def sketch_kernel(
    n, ns, rows, scale, divisor,
    probes_ref, wind_ref, cells_ref, live_ref, weight_ref, out_ref, core_ref,
    ext, recx, slots, first, second, third, total, sums_o, sums_s, parts,
    wind_raw, probes_raw, cells_raw, weight_raw, local_sem, zsend, zrecv, wsend, wrecv, osend, orecv, ssend, srecv, bsend, brecv,
):
    levels, count, columns = ext.shape[1:]
    share = rows // n
    each = count // n
    me = lax.axis_index("obs")
    here = lax.axis_index("space")
    base = me * share
    has_low = here > 0
    has_high = here < ns - 1

    barrier = pltpu.get_barrier_semaphore()
    for j in range(1, n):
        pl.semaphore_signal(
            barrier, inc=1, device_id={"obs": lax.rem(me + j, n)}, device_id_type=MESH
        )
    for j in range(1, ns):
        pl.semaphore_signal(
            barrier, inc=1, device_id={"space": lax.rem(here + j, ns)}, device_id_type=MESH
        )
    depth = wind_ref.shape[0]
    need_low = base < REACH
    need_high = (n - 1 - me) * share < REACH
    load_winds = pltpu.make_async_copy(wind_ref, wind_raw, local_sem.at[0])
    load_probes = pltpu.make_async_copy(probes_ref, probes_raw, local_sem.at[1])
    load_cells = pltpu.make_async_copy(cells_ref, cells_raw, local_sem.at[2])
    load_weight = pltpu.make_async_copy(weight_ref, weight_raw, local_sem.at[3])
    for load in (load_cells, load_weight, load_winds, load_probes):
        load.start()

    @pl.when(jnp.logical_not(has_low))
    def _():
        recx[pl.ds(0, WIND_REACH)] = jnp.zeros((WIND_REACH,) + recx.shape[1:], jnp.float32)
        for r in range(REACH):
            ext[r] = jnp.zeros(ext.shape[1:], jnp.float32)

    @pl.when(jnp.logical_not(has_high))
    def _():
        recx[pl.ds(WIND_REACH + rows, WIND_REACH)] = jnp.zeros(
            (WIND_REACH,) + recx.shape[1:], jnp.float32
        )
        for r in range(REACH):
            ext[REACH + rows + r] = jnp.zeros(ext.shape[1:], jnp.float32)

    load_cells.wait()
    load_weight.wait()
    cells = cells_raw[...]
    slot_count = cells.shape[1]
    slot = lax.broadcasted_iota(jnp.int32, (1, slot_count), 1)
    weight = jnp.where(slot < live_ref[0, 0], weight_raw[...], 0.0)
    line = lax.broadcasted_iota(jnp.int32, (rows * levels, slot_count), 0)
    start = (lax.rem(line, levels) * rows + lax.div(line, levels)) * columns
    on_line = jnp.logical_and(cells >= start, cells < start + columns)
    at_column = lax.rem(cells, columns) == lax.broadcasted_iota(
        jnp.int32, (columns, slot_count), 0
    )
    weights = dot_t(
        jnp.where(on_line, weight, 0.0), jnp.where(at_column, 1.0, 0.0).astype(jnp.float32)
    )
    for r in range(rows):
        recx[WIND_REACH + r, pl.ds(depth, levels)] = weights[r * levels : (r + 1) * levels]
    total[...] = jnp.zeros_like(total)
    load_winds.wait()
    recx[pl.ds(WIND_REACH, rows), pl.ds(0, depth)] = jnp.swapaxes(wind_raw[...], 0, 1)

    pl.semaphore_wait(barrier, n - 1 + ns - 1)

    up = {"space": lax.rem(here + 1, ns)}
    down = {"space": lax.rem(here + ns - 1, ns)}

    def z_copy(index, source, target, device):
        return pltpu.make_async_remote_copy(
            src_ref=source, dst_ref=target, send_sem=zsend.at[index], recv_sem=zrecv.at[index],
            device_id=device, device_id_type=MESH,
        )

    rec_up = z_copy(
        0, recx.at[pl.ds(rows, WIND_REACH)], recx.at[pl.ds(0, WIND_REACH)], up
    )
    rec_down = z_copy(
        1, recx.at[pl.ds(WIND_REACH, WIND_REACH)],
        recx.at[pl.ds(WIND_REACH + rows, WIND_REACH)], down,
    )
    probes_up = [
        z_copy(2 + h, ext.at[rows + h], ext.at[h], up) for h in range(REACH)
    ]
    probes_down = [
        z_copy(2 + REACH + h, ext.at[REACH + h], ext.at[REACH + rows + h], down)
        for h in range(REACH)
    ]
    sends_up = jnp.logical_and(has_high, need_low)
    sends_down = jnp.logical_and(has_low, need_high)
    pl.when(has_high)(rec_up.start)
    pl.when(has_low)(rec_down.start)
    load_probes.wait()
    for lev in range(levels):
        ext[pl.ds(REACH, rows), lev] = jnp.swapaxes(probes_raw[:, lev], 0, 1)
    for copy in reversed(probes_up):
        pl.when(sends_up)(copy.start)
    for copy in probes_down:
        pl.when(sends_down)(copy.start)

    span = share + 2 * WIND_REACH

    def other(j):
        if n & (n - 1):
            return lax.rem(me + j, n)
        peer, bit = me, 1
        while bit < n:
            if j & bit:
                peer = peer + bit * (1 - 2 * lax.rem(me // bit, 2))
            bit *= 2
        return peer

    def w_copy(j):
        peer = other(j)
        slot = j if not n & (n - 1) else n - j
        return pltpu.make_async_remote_copy(
            src_ref=recx.at[pl.ds(peer * share, span)], dst_ref=slots.at[slot],
            send_sem=wsend.at[j], recv_sem=wrecv.at[slot],
            device_id={"obs": peer}, device_id_type=MESH,
        )

    gets_low = jnp.logical_and(has_low, need_low)
    gets_high = jnp.logical_and(has_high, need_high)

    column = lax.broadcasted_iota(jnp.int32, (levels, columns), 1)
    inside_right = column < columns - 1
    inside_left = column > 0

    def valid(row):
        at = here * rows + row
        return jnp.where(jnp.logical_and(at >= 0, at < ns * rows), 1.0, 0.0).astype(jnp.float32)

    def own_wind(row, which):
        return recx[base + row, pl.ds(which * levels, levels), :]

    def wind_in(j):
        return lambda row, which: slots[j, row, pl.ds(which * levels, levels), :]

    def advance(upper, centre, lower, cu, cd, cr, cl, keep, finish):
        cr = jnp.where(inside_right, cr, 0.0) * keep
        cl = jnp.where(inside_left, cl, 0.0) * keep
        cu = cu * keep
        cd = cd * keep
        mid = 0.2 * keep
        vertical = 0.1 * keep
        for lev in range(levels):
            u = centre[lev]
            if levels == 1:
                beside = jnp.zeros_like(u)
            elif lev == 0:
                beside = centre[1]
            elif lev == levels - 1:
                beside = centre[lev - 1]
            else:
                beside = centre[lev - 1] + centre[lev + 1]
            value = (
                mid * u
                + vertical * beside
                + cu[lev : lev + 1] * upper[lev]
                + cd[lev : lev + 1] * lower[lev]
                + cr[lev : lev + 1] * pltpu.roll(u, columns - 1, 1)
                + cl[lev : lev + 1] * pltpu.roll(u, 1, 1)
            )
            finish(lev, value)

    def forward_1(wind_of, k):
        at = base + k + 1
        a, b = 0.5 * wind_of(k, 0), 0.5 * wind_of(k, 1)

        def finish(lev, value):
            first[k, lev] = value

        advance(
            ext.at[at + 1], ext.at[at], ext.at[at - 1],
            0.15 - a, 0.15 + a, 0.15 - b, 0.15 + b, valid(base + k - 3), finish,
        )

    def forward_2(wind_of, k):
        a, b = 0.5 * wind_of(k + 1, 2), 0.5 * wind_of(k + 1, 3)
        weight = wind_of(k + 1, 4)

        def finish(lev, value):
            second[k, lev] = value * weight[lev : lev + 1]

        advance(
            first.at[k + 2], first.at[k + 1], first.at[k],
            0.15 - a, 0.15 + a, 0.15 - b, 0.15 + b, jnp.float32(1.0), finish,
        )

    def across(b):
        return 0.15 + pltpu.roll(b, columns - 1, 1), 0.15 - pltpu.roll(b, 1, 1)

    def adjoint_1(wind_of, k):
        cr, cl = across(0.5 * wind_of(k + 2, 3))

        def finish(lev, value):
            third[k, lev] = value

        advance(
            second.at[k + 2], second.at[k + 1], second.at[k],
            0.15 + 0.5 * wind_of(k + 3, 2), 0.15 - 0.5 * wind_of(k + 1, 2),
            cr, cl, valid(base + k - 1), finish,
        )

    def adjoint_2(wind_of, k):
        cr, cl = across(0.5 * wind_of(k + 3, 1))

        def finish(lev, value):
            total[k, lev] += value

        advance(
            third.at[k + 2], third.at[k + 1], third.at[k],
            0.15 + 0.5 * wind_of(k + 4, 0), 0.15 - 0.5 * wind_of(k + 2, 0),
            cr, cl, jnp.float32(1.0), finish,
        )

    both_sides = jnp.logical_and(need_low, need_high)
    ready = span
    for at in (p * share for p in range(n)):
        if at < REACH:
            ready = min(ready, span - (REACH - at))
        if (n - 1) * share - at < REACH:
            ready = min(ready, REACH + rows - 2 - at)
    wavefront = ready >= 6

    def place(i, stage):
        return jnp.where(need_low, span - 1 - i, i - 2 * stage)

    unroll = 2 if share % 2 == 0 else 1
    later = ((2, forward_2), (4, adjoint_1), (6, adjoint_2))

    def local_row(i, c):
        forward_1(own_wind, place(i, 0))
        return c

    def later_sweeps(end):
        for begin, step in later:

            def body(i, c):
                step(own_wind, place(i, begin // 2))
                return c

            if begin < end:
                lax.fori_loop(begin, end, body, 0, unroll=unroll)

    def arriving(i, c):
        k = place(i, 0)
        for h in range(REACH):
            pl.when(jnp.logical_and(gets_low, base + k == h))(probes_up[h].wait_recv)
            pl.when(
                jnp.logical_and(
                    jnp.logical_and(gets_high, jnp.logical_not(both_sides)),
                    base + k + 2 == REACH + rows + h,
                )
            )(probes_down[h].wait_recv)
        forward_1(own_wind, k)
        if wavefront:
            for begin, step in later:
                step(own_wind, place(i, begin // 2))
        return c

    if wavefront:
        lax.fori_loop(0, ready, local_row, 0, unroll=unroll)

    pl.when(has_low)(rec_up.wait_recv)
    pl.when(has_high)(rec_down.wait_recv)
    winds = [w_copy(j) for j in range(1, n)]
    for copy in winds:
        copy.start()

    if wavefront:
        later_sweeps(ready)
    for h in range(REACH):
        pl.when(jnp.logical_and(gets_high, both_sides))(probes_down[h].wait_recv)
    lax.fori_loop(ready if wavefront else 0, span, arriving, 0)
    for h in range(REACH):
        pl.when(jnp.logical_and(gets_low, h < base))(probes_up[h].wait_recv)
        pl.when(
            jnp.logical_and(
                jnp.logical_and(gets_high, jnp.logical_not(both_sides)),
                base + span + 1 < REACH + rows + h,
            )
        )(probes_down[h].wait_recv)

    if not wavefront:
        later_sweeps(span)

    def window(j, carry):
        pltpu.make_async_remote_copy(
            src_ref=recx.at[pl.ds(0, span)], dst_ref=slots.at[j],
            send_sem=wsend.at[j], recv_sem=wrecv.at[j],
            device_id={"obs": lax.rem(me + 1, n)}, device_id_type=MESH,
        ).wait_recv()

        def sweep(step, length):
            def body(k, c):
                step(wind_in(j), k)
                return c

            lax.fori_loop(0, length, body, 0, unroll=unroll)

        sweep(forward_1, share + 6)
        sweep(forward_2, share + 4)
        sweep(adjoint_1, share + 2)
        sweep(adjoint_2, share)
        return carry

    lax.fori_loop(1, n, window, 0)

    products = jnp.zeros((2 * count, count), jnp.float32)
    for k in range(share):
        for lev in range(levels):
            s = total[k, lev]
            both = jnp.concatenate([ext[base + REACH + k, lev], s], axis=0)
            products = products + dot_t(both, s)

    half = count // 2

    def summed(buffer, axis, size, index, send, recv, value):
        buffer[index] = value
        copies = []
        for j in range(1, size):
            peer = lax.rem(index + j, size)
            copies.append(
                pltpu.make_async_remote_copy(
                    src_ref=buffer.at[index], dst_ref=buffer.at[index],
                    send_sem=send.at[j], recv_sem=recv.at[j],
                    device_id={axis: peer}, device_id_type=MESH,
                )
            )
            copies[-1].start()
        for copy in copies:
            copy.wait()
        result = buffer[0]
        for j in range(1, size):
            result = result + buffer[j]
        return result

    packed = jnp.concatenate(
        [products[i * half : (i + 1) * half] for i in (0, 2, 1, 3)], axis=1
    )
    packed = summed(sums_o, "obs", n, me, osend, orecv, packed)
    packed = summed(sums_s, "space", ns, here, ssend, srecv, packed)
    products = jnp.concatenate([packed[:, : 2 * count], packed[:, 2 * count :]], axis=0)
    core_ref[...] = products[:, :count] * (1.0 / divisor)

    row_id = lax.broadcasted_iota(jnp.int32, (count, 2 * count), 0)
    lane_id = lax.broadcasted_iota(jnp.int32, (count, 2 * count), 1)
    work = jnp.where(lane_id < count, jnp.where(lane_id == row_id, 1.0, 0.0), products)
    for k in range(count - 1):
        pivot = work[k : k + 1, :]
        inverse = 1.0 / work[k : k + 1, count + k : count + k + 1]
        factor = jnp.where(row_id > k, work[:, count + k : count + k + 1], 0.0)
        work = work - (factor * pivot) * inverse
    diagonal = jnp.sum(jnp.where(lane_id == row_id + count, work, 0.0), axis=1, keepdims=True)
    inverse = work[:, :count] * (lax.rsqrt(diagonal) * scale)

    copies = []
    for k in range(share):
        for lev in range(levels):
            block = jnp.dot(
                inverse, total[k, lev], precision=HIGHEST, preferred_element_type=jnp.float32
            )
            for p in range(n):
                parts[p, k, lev] = block[p * each : (p + 1) * each]
        for j in range(1, n):
            peer = other(j)
            copy = pltpu.make_async_remote_copy(
                src_ref=parts.at[peer, k], dst_ref=out_ref.at[base + k],
                send_sem=bsend.at[k, j], recv_sem=brecv.at[k, j],
                device_id={"obs": peer}, device_id_type=MESH,
            )
            copy.start()
            copies.append(copy)
        out_ref[base + k] = parts[me, k]

    for copy in copies:
        copy.wait()
    for copy in winds:
        copy.wait_send()
    pl.when(has_high)(rec_up.wait_send)
    pl.when(has_low)(rec_down.wait_send)
    for copy in probes_up:
        pl.when(sends_up)(copy.wait_send)
    for copy in probes_down:
        pl.when(sends_down)(copy.wait_send)


def on_device(probes, wind, station_cell, obs_count, obs_weight):
    count, levels, rows, columns = probes.shape
    n = lax.axis_size("obs")
    ns = lax.axis_size("space")
    slots = station_cell.shape[1]
    share = rows // n
    each = count // n

    steps, components = wind.shape[1:3]
    lines = steps * components * levels
    winds = wind.reshape(lines, rows, columns)
    depth = lines + 8 * pl.cdiv(levels, 8)

    f32 = jnp.float32
    dma = pltpu.SemaphoreType.DMA
    out, core = pl.pallas_call(
        functools.partial(
            sketch_kernel, n, ns, rows, math.sqrt(levels * rows * ns * columns), n * ns * slots
        ),
        out_shape=(
            jax.ShapeDtypeStruct((rows, levels, each, columns), f32),
            jax.ShapeDtypeStruct((count, count), f32),
        ),
        in_specs=[
            pl.BlockSpec(memory_space=pl.ANY),
            pl.BlockSpec(memory_space=pl.ANY),
            pl.BlockSpec(memory_space=pl.ANY),
            pl.BlockSpec(memory_space=pltpu.SMEM),
            pl.BlockSpec(memory_space=pl.ANY),
        ],
        out_specs=(
            pl.BlockSpec(memory_space=pltpu.VMEM),
            pl.BlockSpec(memory_space=pltpu.VMEM),
        ),
        scratch_shapes=[
            pltpu.VMEM((rows + 2 * REACH, levels, count, columns), f32),
            pltpu.VMEM((rows + 2 * WIND_REACH, depth, columns), f32),
            pltpu.VMEM((n, share + 2 * WIND_REACH, depth, columns), f32),
            pltpu.VMEM((share + 6, levels, count, columns), f32),
            pltpu.VMEM((share + 4, levels, count, columns), f32),
            pltpu.VMEM((share + 2, levels, count, columns), f32),
            pltpu.VMEM((share, levels, count, columns), f32),
            pltpu.VMEM((n, count // 2, 4 * count), f32),
            pltpu.VMEM((ns, count // 2, 4 * count), f32),
            pltpu.VMEM((n, share, levels, each, columns), f32),
            pltpu.VMEM((lines, rows, columns), f32),
            pltpu.VMEM((count, levels, rows, columns), f32),
            pltpu.VMEM((1, slots), jnp.int32),
            pltpu.VMEM((1, slots), f32),
            dma((4,)), dma((2 + 2 * REACH,)), dma((2 + 2 * REACH,)), dma((n,)), dma((n,)),
            dma((n,)), dma((n,)), dma((ns,)), dma((ns,)), dma((share, n)), dma((share, n)),
        ],
        compiler_params=pltpu.CompilerParams(
            collective_id=0, has_side_effects=True, vmem_limit_bytes=VMEM_BYTES
        ),
    )(probes, winds, station_cell, obs_count, obs_weight)
    basis = out.transpose(2, 1, 0, 3)
    return basis, core


def solution(mesh):
    in_specs = (
        P(None, None, "space", None),
        P("obs", None, None, None, "space", None),
        P("obs", "space"),
        P("obs", "space"),
        P("obs", "space"),
    )
    out_specs = (P("obs", None, "space", None), P())
    return jax.shard_map(
        on_device, mesh=mesh, in_specs=in_specs, out_specs=out_specs, check_vma=False
    )
```

```python
import functools
import math

import jax
import jax.numpy as jnp
from jax import lax
from jax.experimental import pallas as pl
from jax.experimental.pallas import tpu as pltpu
from jax.sharding import PartitionSpec as P

MESH = pl.DeviceIdType.MESH
REACH = 4
WIND_REACH = REACH - 1
VMEM_BYTES = 64 * 2**20
HIGHEST = lax.Precision.HIGHEST


def dot_t(x, y):
    return lax.dot_general(
        x, y, (((1,), (1,)), ((), ())), precision=HIGHEST, preferred_element_type=jnp.float32
    )


def split(x):
    high = x.astype(jnp.bfloat16)
    rest = x - high.astype(jnp.float32)
    middle = rest.astype(jnp.bfloat16)
    low = (rest - middle.astype(jnp.float32)).astype(jnp.bfloat16)
    return high, middle, low


def sketch_kernel(
    n, ns, rows, scale, divisor,
    probes_ref, wind_ref, cells_ref, live_ref, weight_ref, out_ref, core_ref,
    ext, recx, slots, first, second, third, total, sums_o, sums_s, parts,
    wind_raw, probes_raw, cells_raw, weight_raw, local_sem, zsend, zrecv, wsend, wrecv, osend, orecv, ssend, srecv, bsend, brecv,
):
    levels, count, columns = ext.shape[1:]
    share = rows // n
    each = count // n
    me = lax.axis_index("obs")
    here = lax.axis_index("space")
    base = me * share
    has_low = here > 0
    has_high = here < ns - 1

    barrier = pltpu.get_barrier_semaphore()
    for j in range(1, n):
        pl.semaphore_signal(
            barrier, inc=1, device_id={"obs": lax.rem(me + j, n)}, device_id_type=MESH
        )
    for j in range(1, ns):
        pl.semaphore_signal(
            barrier, inc=1, device_id={"space": lax.rem(here + j, ns)}, device_id_type=MESH
        )
    depth = wind_ref.shape[0]
    need_low = base < REACH
    need_high = (n - 1 - me) * share < REACH
    load_winds = pltpu.make_async_copy(wind_ref, wind_raw, local_sem.at[0])
    load_probes = pltpu.make_async_copy(probes_ref, probes_raw, local_sem.at[1])
    load_cells = pltpu.make_async_copy(cells_ref, cells_raw, local_sem.at[2])
    load_weight = pltpu.make_async_copy(weight_ref, weight_raw, local_sem.at[3])
    for load in (load_cells, load_weight, load_winds, load_probes):
        load.start()

    @pl.when(jnp.logical_not(has_low))
    def _():
        recx[pl.ds(0, WIND_REACH)] = jnp.zeros((WIND_REACH,) + recx.shape[1:], jnp.float32)
        for r in range(REACH):
            ext[r] = jnp.zeros(ext.shape[1:], jnp.float32)

    @pl.when(jnp.logical_not(has_high))
    def _():
        recx[pl.ds(WIND_REACH + rows, WIND_REACH)] = jnp.zeros(
            (WIND_REACH,) + recx.shape[1:], jnp.float32
        )
        for r in range(REACH):
            ext[REACH + rows + r] = jnp.zeros(ext.shape[1:], jnp.float32)

    load_cells.wait()
    load_weight.wait()
    cells = cells_raw[...]
    slot_count = cells.shape[1]
    slot = lax.broadcasted_iota(jnp.int32, (1, slot_count), 1)
    weight = jnp.where(slot < live_ref[0, 0], weight_raw[...], 0.0)
    line = lax.broadcasted_iota(jnp.int32, (rows * levels, slot_count), 0)
    start = (lax.rem(line, levels) * rows + lax.div(line, levels)) * columns
    on_line = jnp.logical_and(cells >= start, cells < start + columns)
    at_column = lax.rem(cells, columns) == lax.broadcasted_iota(
        jnp.int32, (columns, slot_count), 0
    )
    weights = dot_t(
        jnp.where(on_line, weight, 0.0), jnp.where(at_column, 1.0, 0.0).astype(jnp.float32)
    )
    for r in range(rows):
        recx[WIND_REACH + r, pl.ds(depth, levels)] = weights[r * levels : (r + 1) * levels]
    total[...] = jnp.zeros_like(total)
    load_winds.wait()
    recx[pl.ds(WIND_REACH, rows), pl.ds(0, depth)] = jnp.swapaxes(wind_raw[...], 0, 1)

    pl.semaphore_wait(barrier, n - 1 + ns - 1)

    up = {"space": lax.rem(here + 1, ns)}
    down = {"space": lax.rem(here + ns - 1, ns)}

    def z_copy(index, source, target, device):
        return pltpu.make_async_remote_copy(
            src_ref=source, dst_ref=target, send_sem=zsend.at[index], recv_sem=zrecv.at[index],
            device_id=device, device_id_type=MESH,
        )

    rec_up = z_copy(
        0, recx.at[pl.ds(rows, WIND_REACH)], recx.at[pl.ds(0, WIND_REACH)], up
    )
    rec_down = z_copy(
        1, recx.at[pl.ds(WIND_REACH, WIND_REACH)],
        recx.at[pl.ds(WIND_REACH + rows, WIND_REACH)], down,
    )
    probes_up = [
        z_copy(2 + h, ext.at[rows + h], ext.at[h], up) for h in range(REACH)
    ]
    probes_down = [
        z_copy(2 + REACH + h, ext.at[REACH + h], ext.at[REACH + rows + h], down)
        for h in range(REACH)
    ]
    sends_up = jnp.logical_and(has_high, need_low)
    sends_down = jnp.logical_and(has_low, need_high)
    pl.when(has_high)(rec_up.start)
    pl.when(has_low)(rec_down.start)
    load_probes.wait()
    for lev in range(levels):
        ext[pl.ds(REACH, rows), lev] = jnp.swapaxes(probes_raw[:, lev], 0, 1)
    for copy in reversed(probes_up):
        pl.when(sends_up)(copy.start)
    for copy in probes_down:
        pl.when(sends_down)(copy.start)

    span = share + 2 * WIND_REACH

    def other(j):
        if n & (n - 1):
            return lax.rem(me + j, n)
        peer, bit = me, 1
        while bit < n:
            if j & bit:
                peer = peer + bit * (1 - 2 * lax.rem(me // bit, 2))
            bit *= 2
        return peer

    def w_copy(j):
        peer = other(j)
        slot = j if not n & (n - 1) else n - j
        return pltpu.make_async_remote_copy(
            src_ref=recx.at[pl.ds(peer * share, span)], dst_ref=slots.at[slot],
            send_sem=wsend.at[j], recv_sem=wrecv.at[slot],
            device_id={"obs": peer}, device_id_type=MESH,
        )

    gets_low = jnp.logical_and(has_low, need_low)
    gets_high = jnp.logical_and(has_high, need_high)

    column = lax.broadcasted_iota(jnp.int32, (levels, columns), 1)
    inside_right = column < columns - 1
    inside_left = column > 0

    def valid(row):
        at = here * rows + row
        return jnp.where(jnp.logical_and(at >= 0, at < ns * rows), 1.0, 0.0).astype(jnp.float32)

    def own_wind(row, which):
        return recx[base + row, pl.ds(which * levels, levels), :]

    def wind_in(j):
        return lambda row, which: slots[j, row, pl.ds(which * levels, levels), :]

    def advance(upper, centre, lower, cu, cd, cr, cl, keep, finish):
        cr = jnp.where(inside_right, cr, 0.0) * keep
        cl = jnp.where(inside_left, cl, 0.0) * keep
        cu = cu * keep
        cd = cd * keep
        mid = 0.2 * keep
        vertical = 0.1 * keep
        for lev in range(levels):
            u = centre[lev]
            if levels == 1:
                beside = jnp.zeros_like(u)
            elif lev == 0:
                beside = centre[1]
            elif lev == levels - 1:
                beside = centre[lev - 1]
            else:
                beside = centre[lev - 1] + centre[lev + 1]
            value = (
                mid * u
                + vertical * beside
                + cu[lev : lev + 1] * upper[lev]
                + cd[lev : lev + 1] * lower[lev]
                + cr[lev : lev + 1] * pltpu.roll(u, columns - 1, 1)
                + cl[lev : lev + 1] * pltpu.roll(u, 1, 1)
            )
            finish(lev, value)

    def forward_1(wind_of, k):
        at = base + k + 1
        a, b = 0.5 * wind_of(k, 0), 0.5 * wind_of(k, 1)

        def finish(lev, value):
            first[k, lev] = value

        advance(
            ext.at[at + 1], ext.at[at], ext.at[at - 1],
            0.15 - a, 0.15 + a, 0.15 - b, 0.15 + b, valid(base + k - 3), finish,
        )

    def forward_2(wind_of, k):
        a, b = 0.5 * wind_of(k + 1, 2), 0.5 * wind_of(k + 1, 3)
        weight = wind_of(k + 1, 4)

        def finish(lev, value):
            second[k, lev] = value * weight[lev : lev + 1]

        advance(
            first.at[k + 2], first.at[k + 1], first.at[k],
            0.15 - a, 0.15 + a, 0.15 - b, 0.15 + b, jnp.float32(1.0), finish,
        )

    def across(b):
        return 0.15 + pltpu.roll(b, columns - 1, 1), 0.15 - pltpu.roll(b, 1, 1)

    def adjoint_1(wind_of, k):
        cr, cl = across(0.5 * wind_of(k + 2, 3))

        def finish(lev, value):
            third[k, lev] = value

        advance(
            second.at[k + 2], second.at[k + 1], second.at[k],
            0.15 + 0.5 * wind_of(k + 3, 2), 0.15 - 0.5 * wind_of(k + 1, 2),
            cr, cl, valid(base + k - 1), finish,
        )

    def adjoint_2(wind_of, k):
        cr, cl = across(0.5 * wind_of(k + 3, 1))

        def finish(lev, value):
            total[k, lev] += value

        advance(
            third.at[k + 2], third.at[k + 1], third.at[k],
            0.15 + 0.5 * wind_of(k + 4, 0), 0.15 - 0.5 * wind_of(k + 2, 0),
            cr, cl, jnp.float32(1.0), finish,
        )

    both_sides = jnp.logical_and(need_low, need_high)
    ready = span
    for at in (p * share for p in range(n)):
        if at < REACH:
            ready = min(ready, span - (REACH - at))
        if (n - 1) * share - at < REACH:
            ready = min(ready, REACH + rows - 2 - at)
    wavefront = ready >= 6

    def place(i, stage):
        return jnp.where(need_low, span - 1 - i, i - 2 * stage)

    unroll = 2 if share % 2 == 0 else 1
    later = ((2, forward_2), (4, adjoint_1), (6, adjoint_2))

    def local_row(i, c):
        forward_1(own_wind, place(i, 0))
        return c

    def later_sweeps(end):
        for begin, step in later:

            def body(i, c):
                step(own_wind, place(i, begin // 2))
                return c

            if begin < end:
                lax.fori_loop(begin, end, body, 0, unroll=unroll)

    def arriving(i, c):
        k = place(i, 0)
        for h in range(REACH):
            pl.when(jnp.logical_and(gets_low, base + k == h))(probes_up[h].wait_recv)
            pl.when(
                jnp.logical_and(
                    jnp.logical_and(gets_high, jnp.logical_not(both_sides)),
                    base + k + 2 == REACH + rows + h,
                )
            )(probes_down[h].wait_recv)
        forward_1(own_wind, k)
        if wavefront:
            for begin, step in later:
                step(own_wind, place(i, begin // 2))
        return c

    if wavefront:
        lax.fori_loop(0, ready, local_row, 0, unroll=unroll)

    pl.when(has_low)(rec_up.wait_recv)
    pl.when(has_high)(rec_down.wait_recv)
    winds = [w_copy(j) for j in range(1, n)]
    for copy in winds:
        copy.start()

    if wavefront:
        later_sweeps(ready)
    for h in range(REACH):
        pl.when(jnp.logical_and(gets_high, both_sides))(probes_down[h].wait_recv)
    lax.fori_loop(ready if wavefront else 0, span, arriving, 0)
    for h in range(REACH):
        pl.when(jnp.logical_and(gets_low, h < base))(probes_up[h].wait_recv)
        pl.when(
            jnp.logical_and(
                jnp.logical_and(gets_high, jnp.logical_not(both_sides)),
                base + span + 1 < REACH + rows + h,
            )
        )(probes_down[h].wait_recv)

    if not wavefront:
        later_sweeps(span)

    def window(j, carry):
        pltpu.make_async_remote_copy(
            src_ref=recx.at[pl.ds(0, span)], dst_ref=slots.at[j],
            send_sem=wsend.at[j], recv_sem=wrecv.at[j],
            device_id={"obs": lax.rem(me + 1, n)}, device_id_type=MESH,
        ).wait_recv()

        def sweep(step, length):
            def body(k, c):
                step(wind_in(j), k)
                return c

            lax.fori_loop(0, length, body, 0, unroll=unroll)

        sweep(forward_1, share + 6)
        sweep(forward_2, share + 4)
        sweep(adjoint_1, share + 2)
        sweep(adjoint_2, share)
        return carry

    lax.fori_loop(1, n, window, 0)

    products = jnp.zeros((2 * count, count), jnp.float32)
    for k in range(share):
        for lev in range(levels):
            s = split(total[k, lev])
            o = split(ext[base + REACH + k, lev])
            left = jnp.concatenate([o[0], s[0], o[1], s[1], o[2], s[2]], axis=0)
            right = jnp.concatenate(s, axis=0)
            nine = lax.dot_general(
                left, right, (((1,), (1,)), ((), ())), preferred_element_type=jnp.float32
            )
            part = nine[: 2 * count, 2 * count :]
            part = part + nine[2 * count : 4 * count, count : 2 * count]
            part = part + nine[4 * count :, :count]
            part = part + nine[: 2 * count, count : 2 * count]
            part = part + nine[2 * count : 4 * count, :count]
            products = products + (part + nine[: 2 * count, :count])

    half = count // 2

    def summed(buffer, axis, size, index, send, recv, value):
        buffer[index] = value
        copies = []
        for j in range(1, size):
            peer = lax.rem(index + j, size)
            copies.append(
                pltpu.make_async_remote_copy(
                    src_ref=buffer.at[index], dst_ref=buffer.at[index],
                    send_sem=send.at[j], recv_sem=recv.at[j],
                    device_id={axis: peer}, device_id_type=MESH,
                )
            )
            copies[-1].start()
        for copy in copies:
            copy.wait()
        result = buffer[0]
        for j in range(1, size):
            result = result + buffer[j]
        return result

    packed = jnp.concatenate(
        [products[i * half : (i + 1) * half] for i in (0, 2, 1, 3)], axis=1
    )
    packed = summed(sums_o, "obs", n, me, osend, orecv, packed)
    packed = summed(sums_s, "space", ns, here, ssend, srecv, packed)
    products = jnp.concatenate([packed[:, : 2 * count], packed[:, 2 * count :]], axis=0)
    core_ref[...] = products[:, :count] * (1.0 / divisor)

    row_id = lax.broadcasted_iota(jnp.int32, (count, 2 * count), 0)
    lane_id = lax.broadcasted_iota(jnp.int32, (count, 2 * count), 1)
    work = jnp.where(lane_id < count, jnp.where(lane_id == row_id, 1.0, 0.0), products)
    for k in range(count - 1):
        pivot = work[k : k + 1, :]
        inverse = 1.0 / work[k : k + 1, count + k : count + k + 1]
        factor = jnp.where(row_id > k, work[:, count + k : count + k + 1], 0.0)
        work = work - (factor * pivot) * inverse
    diagonal = jnp.sum(jnp.where(lane_id == row_id + count, work, 0.0), axis=1, keepdims=True)
    inverse = work[:, :count] * (lax.rsqrt(diagonal) * scale)

    copies = []
    for k in range(share):
        for lev in range(levels):
            block = jnp.dot(
                inverse, total[k, lev], precision=HIGHEST, preferred_element_type=jnp.float32
            )
            for p in range(n):
                parts[p, k, lev] = block[p * each : (p + 1) * each]
        for j in range(1, n):
            peer = other(j)
            copy = pltpu.make_async_remote_copy(
                src_ref=parts.at[peer, k], dst_ref=out_ref.at[base + k],
                send_sem=bsend.at[k, j], recv_sem=brecv.at[k, j],
                device_id={"obs": peer}, device_id_type=MESH,
            )
            copy.start()
            copies.append(copy)
        out_ref[base + k] = parts[me, k]

    for copy in copies:
        copy.wait()
    for copy in winds:
        copy.wait_send()
    pl.when(has_high)(rec_up.wait_send)
    pl.when(has_low)(rec_down.wait_send)
    for copy in probes_up:
        pl.when(sends_up)(copy.wait_send)
    for copy in probes_down:
        pl.when(sends_down)(copy.wait_send)


def on_device(probes, wind, station_cell, obs_count, obs_weight):
    count, levels, rows, columns = probes.shape
    n = lax.axis_size("obs")
    ns = lax.axis_size("space")
    slots = station_cell.shape[1]
    share = rows // n
    each = count // n

    steps, components = wind.shape[1:3]
    lines = steps * components * levels
    winds = wind.reshape(lines, rows, columns)
    depth = lines + 8 * pl.cdiv(levels, 8)

    f32 = jnp.float32
    dma = pltpu.SemaphoreType.DMA
    out, core = pl.pallas_call(
        functools.partial(
            sketch_kernel, n, ns, rows, math.sqrt(levels * rows * ns * columns), n * ns * slots
        ),
        out_shape=(
            jax.ShapeDtypeStruct((rows, levels, each, columns), f32),
            jax.ShapeDtypeStruct((count, count), f32),
        ),
        in_specs=[
            pl.BlockSpec(memory_space=pl.ANY),
            pl.BlockSpec(memory_space=pl.ANY),
            pl.BlockSpec(memory_space=pl.ANY),
            pl.BlockSpec(memory_space=pltpu.SMEM),
            pl.BlockSpec(memory_space=pl.ANY),
        ],
        out_specs=(
            pl.BlockSpec(memory_space=pltpu.VMEM),
            pl.BlockSpec(memory_space=pltpu.VMEM),
        ),
        scratch_shapes=[
            pltpu.VMEM((rows + 2 * REACH, levels, count, columns), f32),
            pltpu.VMEM((rows + 2 * WIND_REACH, depth, columns), f32),
            pltpu.VMEM((n, share + 2 * WIND_REACH, depth, columns), f32),
            pltpu.VMEM((share + 6, levels, count, columns), f32),
            pltpu.VMEM((share + 4, levels, count, columns), f32),
            pltpu.VMEM((share + 2, levels, count, columns), f32),
            pltpu.VMEM((share, levels, count, columns), f32),
            pltpu.VMEM((n, count // 2, 4 * count), f32),
            pltpu.VMEM((ns, count // 2, 4 * count), f32),
            pltpu.VMEM((n, share, levels, each, columns), f32),
            pltpu.VMEM((lines, rows, columns), f32),
            pltpu.VMEM((count, levels, rows, columns), f32),
            pltpu.VMEM((1, slots), jnp.int32),
            pltpu.VMEM((1, slots), f32),
            dma((4,)), dma((2 + 2 * REACH,)), dma((2 + 2 * REACH,)), dma((n,)), dma((n,)),
            dma((n,)), dma((n,)), dma((ns,)), dma((ns,)), dma((share, n)), dma((share, n)),
        ],
        compiler_params=pltpu.CompilerParams(
            collective_id=0, has_side_effects=True, vmem_limit_bytes=VMEM_BYTES
        ),
    )(probes, winds, station_cell, obs_count, obs_weight)
    basis = out.transpose(2, 1, 0, 3)
    return basis, core


def solution(mesh):
    in_specs = (
        P(None, None, "space", None),
        P("obs", None, None, None, "space", None),
        P("obs", "space"),
        P("obs", "space"),
        P("obs", "space"),
    )
    out_specs = (P("obs", None, "space", None), P())
    return jax.shard_map(
        on_device, mesh=mesh, in_specs=in_specs, out_specs=out_specs, check_vma=False
    )
```
